256 devices in a mesh: frame: 32 (over z, y_hi, core), pix: 8 (over x, y_lo).
Axes of the slice: x: 4, y: 4 (y_hi: 2, y_lo: 2; y = y_hi * 2 + y_lo), z: 8, core: 2. Of those that a mesh axis runs over, the one named last changes fastest.
Arguments:
- library: float32 [12288, 3072], P('frame', 'pix'), may hold values from -5000 to 5000
- annulus: int32 [1536], P('pix'), may hold values from 0 to 383, as said below
Outputs:
- gram: float32 [12288, 12288], P('frame', 'pix')
The draws below stay inside these ranges and needn't reach their ends.
Inputs may be any that keep to these rules, and one draw needn't show every extreme that they name: `annulus`: within each aligned block of 192 entries the values are distinct and rising, and each block holds both 0 and 383.
All inputs are finite; a program needn't handle non-finite values.
Results may differ from the reference program's by a relative error of at most 0.000065.
Values sent between devices are 32-bit elements; how exact they have to be, the bound alone decides.
A program may use at most 128 MiB of HBM per device.

```python
import math
import jax
import jax.numpy as jnp
from jax import lax

PIX = 1536
PIX_DEV = 192
BAND_DEV = 384
BAND = 3072
FRAMES = 12288
N_PIX = 8


def draw_library(key, part):
    key = jax.random.fold_in(key, 11)
    keys = jax.random.split(key, 6)
    frame_scale = jnp.exp(jax.random.uniform(keys[0], (FRAMES,), jnp.float32) * math.log(10.0))
    column_rise = jnp.power(3.0, jnp.arange(BAND, dtype=jnp.float32) / (BAND - 1))
    column_amp = column_rise * jnp.exp(jax.random.uniform(keys[1], (BAND,), jnp.float32) * math.log(10.0))
    speckle = jnp.clip(jax.random.normal(keys[2], (BAND,), jnp.float32), -4.0, 4.0)
    offset = jnp.clip(jax.random.normal(keys[3], (FRAMES,), jnp.float32), -4.0, 4.0)
    common = jnp.clip(jax.random.normal(keys[4], (FRAMES,), jnp.float32), -4.0, 4.0)
    noise = jnp.clip(jax.random.normal(keys[5], (FRAMES, BAND), jnp.float32), -5.0, 5.0)
    inner = common[:, None] * speckle[None, :] + noise
    return frame_scale[:, None] * (offset[:, None] + column_amp[None, :] * inner)


def draw_annulus(key, part):
    key = jax.random.fold_in(key, 23)
    blocks = PIX // PIX_DEV
    block_keys = jax.random.split(key, blocks)

    def one_block(block_key):
        order = jax.random.permutation(block_key, BAND_DEV - 2).astype(jnp.int32) + 1
        chosen = order[:PIX_DEV - 2]
        ends = jnp.array([0, BAND_DEV - 1], dtype=jnp.int32)
        return jnp.sort(jnp.concatenate([ends, chosen]))
    return jax.vmap(one_block)(block_keys).reshape(PIX).astype(jnp.int32)


def setup_inputs(seed: int = 0) -> dict:
    splits = jax.random.split(jax.random.key(seed), 3)
    return {
        "library": draw_library(jax.random.fold_in(splits[2], 71), 0),
        "annulus": draw_annulus(jax.random.fold_in(splits[2], 71), 0),
    }


def reference(library, annulus):
    banded = library.reshape(FRAMES, N_PIX, BAND_DEV)
    where = jnp.broadcast_to(annulus.reshape(1, N_PIX, PIX_DEV), (FRAMES, N_PIX, PIX_DEV))
    picked = jnp.take_along_axis(banded, where, axis=2).reshape(FRAMES, PIX)
    frame_mean = lax.optimization_barrier(jnp.sum(picked, axis=1)) / PIX
    centered = picked - frame_mean[:, None]
    squares = lax.optimization_barrier(jnp.sum(centered * centered, axis=1))
    unit = centered / jnp.sqrt(squares + 1e-06)[:, None]
    return jnp.dot(unit, unit.T, precision=lax.Precision.HIGHEST, preferred_element_type=jnp.float32)
```

```python
import jax
import jax.numpy as jnp
from jax import lax
from jax.experimental import pallas as pl
from jax.experimental.pallas import tpu as pltpu
from jax.sharding import PartitionSpec as P

PIX = 1536
NZ = 8
NPIX = 8
SL = 24
ROWS = NZ * SL
FR = 384
NA = 4
EPS = 1e-06
MESH = pl.DeviceIdType.MESH
F32 = jnp.float32
BF16 = jnp.bfloat16


def device(x, y, z, c):
    return (z * 4 + (y // 2) * 2 + c, x * 2 + y % 2)


def split(v):
    hi = v.astype(BF16)
    return hi, (v - hi.astype(F32)).astype(BF16)


def dot(a, b):
    return lax.dot_general(a, b, (((1,), (0,)), ((), ())), preferred_element_type=F32)


def kernel(
    lib_ref, ann_ref, out_ref,
    piece, part, rows, cols, acc, mu, s1, s2, rmean, rscale,
    snd, scat, move, ag0, ag1, bex, rowsem, sibrow, outsem, outsnd,
):
    f = lax.axis_index("frame")
    p = lax.axis_index("pix")
    z, yh, c = f // 4, (f // 2) % 2, f % 2
    x, yl = p // 2, p % 2
    y = 2 * yh + yl

    def at(dx=0, dy=0, dz=0, dc=0):
        return device((x + dx) % 4, (y + dy) % 4, (z + dz) % NZ, (c + dc) % 2)

    sibling = at(dc=1)
    partner = at(dy=2)
    flip = device(x, 2 * yh + 1 - yl, z, c)
    pf = 2 * x + 1 - yl

    barrier = pltpu.get_barrier_semaphore()
    for d in range(1, NZ):
        pl.semaphore_signal(barrier, inc=1, device_id=at(dz=d), device_id_type=MESH)
    for dx in range(4):
        for dy in range(4):
            if dx or dy:
                pl.semaphore_signal(barrier, inc=1, device_id=at(dx, dy), device_id_type=MESH)
    pl.semaphore_signal(barrier, inc=1, device_id=sibling, device_id_type=MESH)

    band = lax.broadcasted_iota(jnp.int32, (FR, ROWS), 0)
    onehot = jnp.where(band == ann_ref[...], 1.0, 0.0).astype(F32).T.astype(BF16)
    lib = lib_ref[...]
    hi = lib.astype(BF16)
    rest = lib - hi.astype(F32)
    mid = rest.astype(BF16)
    low = (rest - mid.astype(F32)).astype(BF16)
    nt = (((1,), (1,)), ((), ()))
    picked = lax.dot_general(onehot, hi, nt, preferred_element_type=F32)
    picked += lax.dot_general(onehot, mid, nt, preferred_element_type=F32)
    picked += lax.dot_general(onehot, low, nt, preferred_element_type=F32)
    picked = picked.reshape(NZ, SL, FR)
    piece[...] = picked
    rows[c, :, p] = picked

    pl.semaphore_wait(barrier, 23)

    def send(src, dst, out, into, to):
        pltpu.make_async_remote_copy(
            src_ref=src, dst_ref=dst, send_sem=out, recv_sem=into, device_id=to, device_id_type=MESH
        ).start()

    def wait(like, sem):
        pltpu.make_async_copy(like, like, sem).wait()

    for d in (1, 7, 2, 6, 3, 5, 4):
        w = (z + d) % NZ
        send(piece.at[w], part.at[z], snd.at[0], scat.at[z], at(dz=d))

    send(piece, rows.at[c, :, p], snd.at[1], rowsem.at[p], flip)
    for d in (1, 3, 2):
        send(piece, rows.at[c, :, p], snd.at[1], rowsem.at[p], at(dx=d))
    send(piece, rows.at[c, :, p], snd.at[2], sibrow, sibling)

    def moves(d):
        w = (z + d) % NZ
        if d:
            wait(part.at[w], scat.at[w])
            src = part.at[w]
        else:
            src = piece.at[z]
        near = device(w // 2, w % 2 + 2 * yh, z, c)
        far = device(w // 2, w % 2 + 2 * (1 - yh), z, c)

        @pl.when(w == p)
        def _():
            pltpu.make_async_copy(src, cols.at[z, 0, p], move.at[0]).start()

        @pl.when(w != p)
        def _():
            send(src, cols.at[z, 0, p], snd.at[0], move.at[0], near)

        @pl.when(p < NA)
        def _():
            send(src, cols.at[z, 1, p], snd.at[3], move.at[1], far)

    for d in (0, 1, 7, 2, 6, 3, 5, 4):
        moves(d)

    wait(rows.at[c, :, pf], rowsem.at[pf])
    for d in (1, 3, 2):
        send(rows.at[c, :, pf], rows.at[c, :, pf], snd.at[1], rowsem.at[pf], at(dx=d))
    send(rows.at[c, :, pf], rows.at[c, :, pf], snd.at[2], sibrow, sibling)

    def forward0(j, d):
        send(cols.at[j, 0], cols.at[j, 0], snd.at[4], ag0.at[j], at(dz=d))

    def forward1(j, d):
        a = cols.at[j, 1, pl.ds(0, NA)]
        send(a, a, snd.at[5], ag1.at[j], at(dz=d))

    def cross(j):
        send(
            cols.at[j, 0, pl.ds(NA, NPIX - NA)], cols.at[j, 1, pl.ds(NA, NPIX - NA)],
            snd.at[6], bex.at[j], partner,
        )

    wait(cols.at[z, 0], move.at[0])
    forward0(z, 1)
    forward0(z, 7)
    cross(z)
    wait(cols.at[z, 1, pl.ds(0, NA)], move.at[1])
    forward1(z, 1)
    forward1(z, 7)

    def arrive(t):
        below, above = (z + NZ - t) % NZ, (z + t) % NZ
        if t == 4:
            wait(cols.at[above, 0], ag0.at[above])
            cross(above)
            wait(cols.at[above, 1, pl.ds(0, NA)], ag1.at[above])
            return
        for which, sem, fwd in ((0, ag0, forward0), (1, ag1, forward1)):
            for j, d, core in ((below, 1, 0), (above, 7, 1)):
                if which == 0:
                    wait(cols.at[j, 0], sem.at[j])
                else:
                    wait(cols.at[j, 1, pl.ds(0, NA)], sem.at[j])
                if t < 3:
                    fwd(j, d)
                else:
                    @pl.when(c == core)
                    def _():
                        fwd(j, d)
                if which == 0:
                    cross(j)

    def share(dx, q):
        k = 2 * ((x + dx) % 4) + q
        wait(rows.at[c, :, k], rowsem.at[k])
        send(rows.at[c, :, k], rows.at[c, :, k], snd.at[2], sibrow, sibling)

    arrive(1)
    for d in (1, 3, 2):
        share(d, yl)
    arrive(2)
    for d in (1, 3, 2):
        share(d, 1 - yl)
    arrive(3)
    wait(rows.at[0], sibrow)

    def block(ref, *idx):
        return ref[idx].reshape(ROWS, FR)

    for k in range(2):
        def add(j, tot):
            return tot + jnp.sum(block(rows, k, j), axis=0, keepdims=True)
        mean = lax.fori_loop(0, NZ, add, jnp.zeros((1, FR), F32)) / PIX
        def add2(j, tot):
            v = block(rows, k, j) - mean
            return tot + jnp.sum(v * v, axis=0, keepdims=True)
        sq = lax.fori_loop(0, NZ, add2, jnp.zeros((1, FR), F32))
        rmean[k] = mean
        rscale[k] = 1.0 / jnp.sqrt(sq + EPS)

    def product(j, first):
        if first is False:
            wait(cols.at[j, 1, pl.ds(NA, NPIX - NA)], bex.at[j])
        rhs = []
        for h in range(2):
            v = block(cols, j, h)
            if first:
                mu[h] = jnp.sum(v, axis=0, keepdims=True) / ROWS
            v = v - mu[h]
            one = jnp.sum(v, axis=0, keepdims=True)
            two = jnp.sum(v * v, axis=0, keepdims=True)
            if first:
                s1[h] = one
                s2[h] = two
            else:
                s1[h] += one
                s2[h] += two
            rhs.append(split(v))
        for k in range(2):
            u = (block(rows, k, j) - rmean[k]) * rscale[k]
            uhi, ulo = split(u)
            uhi, ulo = uhi.T, ulo.T
            for h in range(2):
                xhi, xlo = rhs[h]
                r = dot(uhi, xhi) + dot(uhi, xlo) + dot(ulo, xhi)
                if first:
                    acc[h, k] = r
                else:
                    acc[h, k] += r

    wait(cols.at[z, 1, pl.ds(NA, NPIX - NA)], bex.at[z])
    product(z, True)

    arrive(4)

    @pl.loop(1, NZ)
    def _(i):
        d = jnp.where(i % 2 == 1, (i + 1) // 2, NZ - i // 2)
        product((z + d) % NZ, False)

    copies = []
    for h in range(2):
        m = s1[h] / PIX
        sq = jnp.maximum(s2[h] - PIX * m * m, 0.0)
        r = 1.0 / jnp.sqrt(sq + EPS)
        col = pl.multiple_of((2 * (yh if h == 0 else 1 - yh) + c) * FR, 128)
        here = out_ref.at[:, pl.ds(col, FR)]
        acc[h, 1 - c] = acc[h, 1 - c] * r
        theirs = pltpu.make_async_remote_copy(
            src_ref=acc.at[h, 1 - c], dst_ref=here, send_sem=outsnd.at[h], recv_sem=outsem.at[h],
            device_id=sibling, device_id_type=MESH,
        )
        theirs.start()
        acc[h, c] = acc[h, c] * r
        mine = pltpu.make_async_copy(acc.at[h, c], here, outsnd.at[2 + h])
        mine.start()
        copies.append((theirs, mine))
    for theirs, mine in copies:
        theirs.wait()
        mine.wait()

    wait(cols.at[pl.ds(0, 7), 0, pl.ds(0, 2)], snd.at[0])
    wait(cols.at[pl.ds(0, 7), 0], snd.at[1])
    wait(cols.at[:, 0], snd.at[2])

    @pl.when(p < NA)
    def _():
        wait(cols.at[0, 0], snd.at[3])

    wait(cols.at[pl.ds(0, 7), 0], snd.at[4])
    wait(cols.at[pl.ds(0, 7), 0, pl.ds(0, NA)], snd.at[5])
    wait(cols.at[:, 0, pl.ds(0, NPIX - NA)], snd.at[6])


def local(library, annulus):
    dma = pltpu.SemaphoreType.DMA
    return pl.pallas_call(
        kernel,
        out_shape=jax.ShapeDtypeStruct((FR, 4 * FR), F32),
        in_specs=[pl.BlockSpec(memory_space=pltpu.VMEM)] * 2,
        out_specs=pl.BlockSpec(memory_space=pl.ANY),
        scratch_shapes=[
            pltpu.VMEM((NZ, SL, FR), F32),
            pltpu.VMEM((NZ, SL, FR), F32),
            pltpu.VMEM((2, NZ, NPIX, SL, FR), F32),
            pltpu.VMEM((NZ, 2, NPIX, SL, FR), F32),
            pltpu.VMEM((2, 2, FR, FR), F32),
            pltpu.VMEM((2, 1, FR), F32),
            pltpu.VMEM((2, 1, FR), F32),
            pltpu.VMEM((2, 1, FR), F32),
            pltpu.VMEM((2, 1, FR), F32),
            pltpu.VMEM((2, 1, FR), F32),
            dma((7,)),
            dma((NZ,)),
            dma((2,)),
            dma((NZ,)),
            dma((NZ,)),
            dma((NZ,)),
            dma((NPIX,)),
            dma,
            dma((2,)),
            dma((4,)),
        ],
        compiler_params=pltpu.CompilerParams(
            collective_id=0, has_side_effects=True, vmem_limit_bytes=48 * 2**20
        ),
    )(library, annulus.reshape(1, ROWS))


def solution(mesh):
    placed = (P("frame", "pix"), P("pix"))
    return jax.shard_map(
        local, mesh=mesh, in_specs=placed, out_specs=P("frame", "pix"), check_vma=False
    )
```

```python
import jax
import jax.numpy as jnp
from jax import lax
from jax.experimental import pallas as pl
from jax.experimental.pallas import tpu as pltpu
from jax.sharding import PartitionSpec as P

PIX = 1536
NZ = 8
NPIX = 8
SL = 24
ROWS = NZ * SL
FR = 384
NA = 4
EPS = 1e-06
MESH = pl.DeviceIdType.MESH
F32 = jnp.float32
BF16 = jnp.bfloat16


def device(x, y, z, c):
    return (z * 4 + (y // 2) * 2 + c, x * 2 + y % 2)


def split(v):
    hi = v.astype(BF16)
    return hi, (v - hi.astype(F32)).astype(BF16)


def dot(a, b):
    return lax.dot_general(a, b, (((1,), (0,)), ((), ())), preferred_element_type=F32)


def kernel(
    lib_ref, ann_ref, out_ref,
    piece, rows, cols, acc, mu, s1, s2, rmean, rscale,
    snd, move, ag0, ag1, bex, rowsem, rowlow, sibrow, outsem, outsnd,
):
    f = lax.axis_index("frame")
    p = lax.axis_index("pix")
    z, yh, c = f // 4, (f // 2) % 2, f % 2
    x, yl = p // 2, p % 2
    y = 2 * yh + yl

    def at(dx=0, dy=0, dz=0, dc=0):
        return device((x + dx) % 4, (y + dy) % 4, (z + dz) % NZ, (c + dc) % 2)

    sibling = at(dc=1)
    partner = at(dy=2)
    flip = device(x, 2 * yh + 1 - yl, z, c)
    pf = 2 * x + 1 - yl

    barrier = pltpu.get_barrier_semaphore()
    def greet(to):
        pl.semaphore_signal(barrier, inc=1, device_id=to, device_id_type=MESH)

    def target(w):
        return device(z // 2, z % 2 + 2 * yh, w, c)

    for to in (at(dz=1), at(dz=7), at(dx=1), at(dx=3), flip, partner, sibling):
        greet(to)
    for w in range(NZ):
        @pl.when((w != z) | (z != p))
        def _():
            greet(target(w))
    for k in range(NPIX):
        @pl.when((k != p) | (z != p))
        def _():
            greet(device(k // 2, 2 * yh + k % 2, p, c))

    band = lax.broadcasted_iota(jnp.int32, (FR, ROWS), 0)
    onehot = jnp.where(band == ann_ref[...], 1.0, 0.0).astype(F32).T.astype(BF16)
    lib = lib_ref[...]
    hi = lib.astype(BF16)
    rest = lib - hi.astype(F32)
    mid = rest.astype(BF16)
    low = (rest - mid.astype(F32)).astype(BF16)
    nt = (((1,), (1,)), ((), ()))
    picked = lax.dot_general(onehot, hi, nt, preferred_element_type=F32)
    picked += lax.dot_general(onehot, mid, nt, preferred_element_type=F32)
    picked += lax.dot_general(onehot, low, nt, preferred_element_type=F32)
    picked = picked.reshape(NZ, SL, FR)
    piece[...] = picked
    rows[c, :, p] = picked

    pl.semaphore_wait(barrier, 7 + 2 * NZ - jnp.where(z == p, 2, 0))

    def send(src, dst, out, into, to):
        pltpu.make_async_remote_copy(
            src_ref=src, dst_ref=dst, send_sem=out, recv_sem=into, device_id=to, device_id_type=MESH
        ).start()

    def wait(like, sem):
        pltpu.make_async_copy(like, like, sem).wait()

    def scatter():
        for d in (4, 3, 5, 2, 6, 1, 7):
            w = (z + d) % NZ
            send(piece.at[w], cols.at[w, 0, p], snd.at[0], move, target(w))

        @pl.when(z != p)
        def _():
            send(piece.at[z], cols.at[z, 0, p], snd.at[0], move, target(z))

        @pl.when(z == p)
        def _():
            pltpu.make_async_copy(piece.at[z], cols.at[z, 0, p], move).start()

    def own(j):
        return cols.at[j, 0]

    def also(j):
        return cols.at[j, 1, pl.ds(0, NA)]

    def forward0(j, d):
        send(own(j), own(j), snd.at[4], ag0.at[j], at(dz=d))

    def forward1(j, d):
        send(also(j), also(j), snd.at[5], ag1.at[j], at(dz=d))

    def cross(j):
        rest = pl.ds(NA, NPIX - NA)
        send(cols.at[j, 0, rest], cols.at[j, 1, rest], snd.at[6], bex.at[j], partner)

    def begin():
        wait(own(z), move)
        forward0(z, 1)
        forward0(z, 7)
        send(cols.at[z, 0, pl.ds(0, NA)], also(z), snd.at[3], ag1.at[z], partner)
        cross(z)
        wait(also(z), ag1.at[z])
        forward1(z, 1)
        forward1(z, 7)

    def arrive(t):
        below, above = (z + NZ - t) % NZ, (z + t) % NZ
        for view, sem, fwd in ((own, ag0, forward0), (also, ag1, forward1)):
            for j, d, core in ((below, 1, 0), (above, 7, 1)):
                wait(view(j), sem.at[j])
                if t < 3:
                    fwd(j, d)
                else:
                    @pl.when(c == core)
                    def _():
                        fwd(j, d)
                if view is own:
                    cross(j)

    def row(k):
        return rows.at[c, :, k]

    def share(k):
        send(row(k), row(k), snd.at[2], sibrow, sibling)

    def both(src, k):
        for d in (1, 3):
            send(src, row(k), snd.at[1], rowsem.at[k], at(dx=d))

    def pass_on(q):
        left, right = 2 * ((x + 3) % 4) + q, 2 * ((x + 1) % 4) + q
        wait(row(left), rowsem.at[left])
        top = rows.at[c, pl.ds(0, 4), left]
        send(top, top, snd.at[1], rowsem.at[left], at(dx=1))
        share(left)
        wait(row(right), rowsem.at[right])
        low = rows.at[c, pl.ds(4, 4), right]
        send(low, low, snd.at[1], rowlow.at[right], at(dx=3))
        share(right)

    def last(q):
        k = 2 * ((x + 2) % 4) + q
        wait(rows.at[c, pl.ds(0, 4), k], rowsem.at[k])
        wait(rows.at[c, pl.ds(4, 4), k], rowlow.at[k])
        share(k)

    scatter()
    send(piece, row(p), snd.at[1], rowsem.at[p], flip)
    both(piece, p)
    send(piece, row(p), snd.at[2], sibrow, sibling)
    begin()
    wait(row(pf), rowsem.at[pf])
    both(row(pf), pf)
    share(pf)
    pass_on(yl)
    arrive(1)
    pass_on(1 - yl)
    last(yl)
    arrive(2)
    last(1 - yl)
    wait(rows.at[0], sibrow)

    def block(ref, *idx):
        return ref[idx].reshape(ROWS, FR)

    for k in range(2):
        def add(j, tot):
            return tot + jnp.sum(block(rows, k, j), axis=0, keepdims=True)
        mean = lax.fori_loop(0, NZ, add, jnp.zeros((1, FR), F32)) / PIX
        def add2(j, tot):
            v = block(rows, k, j) - mean
            return tot + jnp.sum(v * v, axis=0, keepdims=True)
        sq = lax.fori_loop(0, NZ, add2, jnp.zeros((1, FR), F32))
        rmean[k] = mean
        rscale[k] = 1.0 / jnp.sqrt(sq + EPS)

    def shifted(j, h, first):
        v = block(cols, j, h)
        if first:
            mu[h] = jnp.sum(v, axis=0, keepdims=True) / ROWS
        v = v - mu[h]
        one = jnp.sum(v, axis=0, keepdims=True)
        two = jnp.sum(v * v, axis=0, keepdims=True)
        s1[h] = one if first else s1[h] + one
        s2[h] = two if first else s2[h] + two
        return split(v)

    def product(j, hs, first=False):
        if 1 in hs:
            wait(cols.at[j, 1, pl.ds(NA, NPIX - NA)], bex.at[j])
        pairs = [shifted(j, h, first) for h in hs]
        xhi, xlo = (jnp.concatenate(v, axis=1) for v in zip(*pairs))
        for k in range(2):
            u = (block(rows, k, j) - rmean[k]) * rscale[k]
            uhi, ulo = split(u)
            uhi, ulo = uhi.T, ulo.T
            r = dot(uhi, xhi) + dot(uhi, xlo) + dot(ulo, xhi)
            for i, h in enumerate(hs):
                r_h = r[:, i * FR : (i + 1) * FR]
                acc[h, k] = r_h if first else acc[h, k] + r_h

    def pair(t):
        @pl.loop(0, 2)
        def _(i):
            product((z + jnp.where(i == 0, t, NZ - t)) % NZ, (0, 1))

    copies = []

    def output(h):
        m = s1[h] / PIX
        sq = jnp.maximum(s2[h] - PIX * m * m, 0.0)
        r = 1.0 / jnp.sqrt(sq + EPS)
        col = pl.multiple_of((2 * (yh if h == 0 else 1 - yh) + c) * FR, 128)
        here = out_ref.at[:, pl.ds(col, FR)]
        acc[h, 1 - c] = acc[h, 1 - c] * r
        theirs = pltpu.make_async_remote_copy(
            src_ref=acc.at[h, 1 - c], dst_ref=here, send_sem=outsnd.at[h], recv_sem=outsem.at[h],
            device_id=sibling, device_id_type=MESH,
        )
        theirs.start()
        acc[h, c] = acc[h, c] * r
        mine = pltpu.make_async_copy(acc.at[h, c], here, outsnd.at[2 + h])
        mine.start()
        copies.append((theirs, mine))

    far = (z + 4) % NZ
    product(z, (0, 1), True)
    pair(1)
    arrive(3)
    pair(2)
    wait(own(far), ag0.at[far])
    cross(far)
    pair(3)
    product(far, (0,))
    output(0)
    wait(also(far), ag1.at[far])
    product(far, (1,))
    output(1)
    for theirs, mine in copies:
        theirs.wait()
        mine.wait()

    wait(cols.at[0, 0, pl.ds(0, 7)], snd.at[0])

    @pl.when(z != p)
    def _():
        wait(piece.at[0], snd.at[0])

    wait(cols.at[pl.ds(0, 7), 0], snd.at[1])
    wait(cols.at[:, 0], snd.at[2])

    wait(also(0), snd.at[3])
    wait(cols.at[pl.ds(0, 7), 0], snd.at[4])
    wait(cols.at[pl.ds(0, 7), 0, pl.ds(0, NA)], snd.at[5])
    wait(cols.at[:, 0, pl.ds(0, NPIX - NA)], snd.at[6])


def local(library, annulus):
    dma = pltpu.SemaphoreType.DMA
    return pl.pallas_call(
        kernel,
        out_shape=jax.ShapeDtypeStruct((FR, 4 * FR), F32),
        in_specs=[pl.BlockSpec(memory_space=pltpu.VMEM)] * 2,
        out_specs=pl.BlockSpec(memory_space=pl.ANY),
        scratch_shapes=[
            pltpu.VMEM((NZ, SL, FR), F32),
            pltpu.VMEM((2, NZ, NPIX, SL, FR), F32),
            pltpu.VMEM((NZ, 2, NPIX, SL, FR), F32),
            pltpu.VMEM((2, 2, FR, FR), F32),
            pltpu.VMEM((2, 1, FR), F32),
            pltpu.VMEM((2, 1, FR), F32),
            pltpu.VMEM((2, 1, FR), F32),
            pltpu.VMEM((2, 1, FR), F32),
            pltpu.VMEM((2, 1, FR), F32),
            dma((7,)),
            dma,
            dma((NZ,)),
            dma((NZ,)),
            dma((NZ,)),
            dma((NPIX,)),
            dma((NPIX,)),
            dma,
            dma((2,)),
            dma((4,)),
        ],
        compiler_params=pltpu.CompilerParams(
            collective_id=0, has_side_effects=True, vmem_limit_bytes=48 * 2**20
        ),
    )(library, annulus.reshape(1, ROWS))


def solution(mesh):
    placed = (P("frame", "pix"), P("pix"))
    return jax.shard_map(
        local, mesh=mesh, in_specs=placed, out_specs=P("frame", "pix"), check_vma=False
    )
```

```python
import jax
import jax.numpy as jnp
from jax import lax
from jax.experimental import pallas as pl
from jax.experimental.pallas import tpu as pltpu
from jax.sharding import PartitionSpec as P

PIX = 1536
NZ = 8
NPIX = 8
SL = 24
ROWS = NZ * SL
FR = 384
EARLY = ((0, 8), (8, 16))
NA = 3
EPS = 1e-06
MESH = pl.DeviceIdType.MESH
F32 = jnp.float32
BF16 = jnp.bfloat16


def device(x, y, z, c):
    return (z * 4 + (y // 2) * 2 + c, x * 2 + y % 2)


def split(v):
    hi = v.astype(BF16)
    return hi, (v - hi.astype(F32)).astype(BF16)


def dot(a, b):
    return lax.dot_general(a, b, (((1,), (0,)), ((), ())), preferred_element_type=F32)


def kernel(
    lib_ref, ann_ref, out_ref,
    piece, rows, cols, acc, mu, s1, s2, rmean, rscale,
    snd, move, ag0, farsem, swap, ag1, bex, rowsem, rowlow, sibrow, outsem, outsnd,
):
    f = lax.axis_index("frame")
    p = lax.axis_index("pix")
    z, yh, c = f // 4, (f // 2) % 2, f % 2
    x, yl = p // 2, p % 2
    y = 2 * yh + yl

    def at(dx=0, dy=0, dz=0, dc=0):
        return device((x + dx) % 4, (y + dy) % 4, (z + dz) % NZ, (c + dc) % 2)

    sibling = at(dc=1)
    partner = at(dy=2)
    flip = device(x, 2 * yh + 1 - yl, z, c)
    pf = 2 * x + 1 - yl

    barrier = pltpu.get_barrier_semaphore()
    def greet(to):
        pl.semaphore_signal(barrier, inc=1, device_id=to, device_id_type=MESH)

    def target(w):
        return device(z // 2, z % 2 + 2 * yh, w, c)

    for to in (at(dz=1), at(dz=7), at(dx=1), at(dx=3), flip, partner, sibling):
        greet(to)
    for w in range(NZ):
        @pl.when((w != z) | (z != p))
        def _():
            greet(target(w))
    for k in range(NPIX):
        @pl.when((k != p) | (z != p))
        def _():
            greet(device(k // 2, 2 * yh + k % 2, p, c))

    band = lax.broadcasted_iota(jnp.int32, (FR, ROWS), 0)
    onehot = jnp.where(band == ann_ref[...], 1.0, 0.0).astype(F32).T.astype(BF16)
    lib = lib_ref[...]
    hi = lib.astype(BF16)
    rest = lib - hi.astype(F32)
    mid = rest.astype(BF16)
    low = (rest - mid.astype(F32)).astype(BF16)
    nt = (((1,), (1,)), ((), ()))
    picked = lax.dot_general(onehot, hi, nt, preferred_element_type=F32)
    picked += lax.dot_general(onehot, mid, nt, preferred_element_type=F32)
    picked += lax.dot_general(onehot, low, nt, preferred_element_type=F32)
    picked = picked.reshape(NZ, SL, FR)
    piece[...] = picked
    rows[c, :, p] = picked

    pl.semaphore_wait(barrier, 7 + 2 * NZ - jnp.where(z == p, 2, 0))

    def send(src, dst, out, into, to):
        pltpu.make_async_remote_copy(
            src_ref=src, dst_ref=dst, send_sem=out, recv_sem=into, device_id=to, device_id_type=MESH
        ).start()

    def wait(like, sem):
        pltpu.make_async_copy(like, like, sem).wait()

    def scatter(g):
        span = pl.ds(*EARLY[g])
        for d in (4, 3, 5, 2, 6, 1, 7):
            w = (z + d) % NZ
            send(piece.at[w, span], cols.at[w, 0, p, span], snd.at[0], move.at[g], target(w))

        @pl.when(z != p)
        def _():
            send(piece.at[z, span], cols.at[z, 0, p, span], snd.at[0], move.at[g], target(z))

        @pl.when(z == p)
        def _():
            pltpu.make_async_copy(piece.at[z, span], cols.at[z, 0, p, span], move.at[g]).start()

    late, soon = pl.ds(NA, NPIX - NA), pl.ds(0, NA)

    def b(j):
        return cols.at[j, 0, late]

    def a(j):
        return cols.at[j, :, soon]

    def cross(j):
        send(b(j), cols.at[j, 1, late], snd.at[6], bex.at[j], partner)

    def begin():
        for g in range(len(EARLY)):
            span = pl.ds(*EARLY[g])
            wait(cols.at[z, 0, :, span], move.at[g])
            part = cols.at[z, 0, late, span]
            for d in (1, 7):
                send(part, part, snd.at[4], ag0.at[z], at(dz=d))
        send(cols.at[z, 0, soon], cols.at[z, 1, soon], snd.at[3], swap, partner)
        cross(z)

    def swapped():
        wait(cols.at[z, 1, soon], swap)
        for d in (1, 7):
            send(a(z), a(z), snd.at[5], ag1.at[z], at(dz=d))

    def ends(t):
        return ((z + NZ - t) % NZ, 1, 0), ((z + t) % NZ, 7, 1)

    def arrive_b(t):
        for j, d, core in ends(t):
            wait(b(j), ag0.at[j])
            if t < 3:
                send(b(j), b(j), snd.at[4], ag0.at[j], at(dz=d))
            else:
                @pl.when(c == core)
                def _():
                    send(b(j), b(j), snd.at[4], ag0.at[j], at(dz=d))
            cross(j)

    def arrive_a(t):
        for j, d, core in ends(t):
            wait(a(j), ag1.at[j])
            if t < 3:
                send(a(j), a(j), snd.at[5], ag1.at[j], at(dz=d))
            else:
                @pl.when(c == core)
                def _():
                    for h in range(2):
                        part = cols.at[j, h, soon]
                        send(part, part, snd.at[5], farsem.at[h], at(dz=d))

    def row(k):
        return rows.at[c, :, k]

    def share(k):
        send(row(k), row(k), snd.at[2], sibrow, sibling)

    def both(src, k):
        for d in (1, 3):
            send(src, row(k), snd.at[1], rowsem.at[k], at(dx=d))

    def pass_on(q):
        left, right = 2 * ((x + 3) % 4) + q, 2 * ((x + 1) % 4) + q
        wait(row(left), rowsem.at[left])
        top = rows.at[c, pl.ds(0, 4), left]
        send(top, top, snd.at[1], rowsem.at[left], at(dx=1))
        share(left)
        wait(row(right), rowsem.at[right])
        low = rows.at[c, pl.ds(4, 4), right]
        send(low, low, snd.at[1], rowlow.at[right], at(dx=3))
        share(right)

    def last(q):
        k = 2 * ((x + 2) % 4) + q
        wait(rows.at[c, pl.ds(0, 4), k], rowsem.at[k])
        wait(rows.at[c, pl.ds(4, 4), k], rowlow.at[k])
        share(k)

    for g in range(len(EARLY)):
        scatter(g)
    send(piece, row(p), snd.at[1], rowsem.at[p], flip)
    both(piece, p)
    send(piece, row(p), snd.at[2], sibrow, sibling)
    begin()
    wait(row(pf), rowsem.at[pf])
    both(row(pf), pf)
    share(pf)
    pass_on(yl)
    arrive_b(1)
    swapped()
    pass_on(1 - yl)
    arrive_b(2)
    last(yl)
    arrive_a(1)
    arrive_b(3)
    last(1 - yl)
    wait(rows.at[0], sibrow)

    def block(ref, *idx):
        return ref[idx].reshape(ROWS, FR)

    for k in range(2):
        def add(j, tot):
            return tot + jnp.sum(block(rows, k, j), axis=0, keepdims=True)
        mean = lax.fori_loop(0, NZ, add, jnp.zeros((1, FR), F32)) / PIX
        def add2(j, tot):
            v = block(rows, k, j) - mean
            return tot + jnp.sum(v * v, axis=0, keepdims=True)
        sq = lax.fori_loop(0, NZ, add2, jnp.zeros((1, FR), F32))
        rmean[k] = mean
        rscale[k] = 1.0 / jnp.sqrt(sq + EPS)

    def shifted(j, h, first):
        v = block(cols, j, h)
        if first:
            mu[h] = jnp.sum(v, axis=0, keepdims=True) / ROWS
        v = v - mu[h]
        one = jnp.sum(v, axis=0, keepdims=True)
        two = jnp.sum(v * v, axis=0, keepdims=True)
        s1[h] = one if first else s1[h] + one
        s2[h] = two if first else s2[h] + two
        return split(v)

    def product(j, hs, first=False):
        if 1 in hs:
            wait(cols.at[j, 1, late], bex.at[j])
        pairs = [shifted(j, h, first) for h in hs]
        xhi, xlo = (jnp.concatenate(v, axis=1) for v in zip(*pairs))
        for k in range(2):
            u = (block(rows, k, j) - rmean[k]) * rscale[k]
            uhi, ulo = split(u)
            uhi, ulo = uhi.T, ulo.T
            r = dot(uhi, xhi) + dot(uhi, xlo) + dot(ulo, xhi)
            for i, h in enumerate(hs):
                r_h = r[:, i * FR : (i + 1) * FR]
                acc[h, k] = r_h if first else acc[h, k] + r_h

    def pair(t):
        @pl.loop(0, 2)
        def _(i):
            product((z + jnp.where(i == 0, t, NZ - t)) % NZ, (0, 1))

    copies = []

    def output(h):
        m = s1[h] / PIX
        sq = jnp.maximum(s2[h] - PIX * m * m, 0.0)
        r = 1.0 / jnp.sqrt(sq + EPS)
        col = pl.multiple_of((2 * (yh if h == 0 else 1 - yh) + c) * FR, 128)
        here = out_ref.at[:, pl.ds(col, FR)]
        acc[h, 1 - c] = acc[h, 1 - c] * r
        theirs = pltpu.make_async_remote_copy(
            src_ref=acc.at[h, 1 - c], dst_ref=here, send_sem=outsnd.at[h], recv_sem=outsem.at[h],
            device_id=sibling, device_id_type=MESH,
        )
        theirs.start()
        acc[h, c] = acc[h, c] * r
        mine = pltpu.make_async_copy(acc.at[h, c], here, outsnd.at[2 + h])
        mine.start()
        copies.append((theirs, mine))

    far = (z + 4) % NZ
    product(z, (0, 1), True)
    arrive_a(2)
    wait(b(far), ag0.at[far])
    cross(far)
    pair(1)
    pair(2)
    arrive_a(3)
    pair(3)
    wait(cols.at[far, 0, soon], farsem.at[0])
    product(far, (0,))
    output(0)
    wait(cols.at[far, 1, soon], farsem.at[1])
    product(far, (1,))
    output(1)
    for theirs, mine in copies:
        theirs.wait()
        mine.wait()

    wait(cols.at[0, 0, pl.ds(0, 7)], snd.at[0])

    @pl.when(z != p)
    def _():
        wait(piece.at[0], snd.at[0])

    wait(cols.at[pl.ds(0, 7), 0], snd.at[1])
    wait(cols.at[:, 0], snd.at[2])

    wait(cols.at[0, 0, soon], snd.at[3])
    wait(cols.at[pl.ds(0, 7), 0, late], snd.at[4])
    wait(cols.at[pl.ds(0, 7), :, soon], snd.at[5])
    wait(cols.at[:, 0, late], snd.at[6])


def local(library, annulus):
    dma = pltpu.SemaphoreType.DMA
    return pl.pallas_call(
        kernel,
        out_shape=jax.ShapeDtypeStruct((FR, 4 * FR), F32),
        in_specs=[pl.BlockSpec(memory_space=pltpu.VMEM)] * 2,
        out_specs=pl.BlockSpec(memory_space=pl.ANY),
        scratch_shapes=[
            pltpu.VMEM((NZ, SL, FR), F32),
            pltpu.VMEM((2, NZ, NPIX, SL, FR), F32),
            pltpu.VMEM((NZ, 2, NPIX, SL, FR), F32),
            pltpu.VMEM((2, 2, FR, FR), F32),
            pltpu.VMEM((2, 1, FR), F32),
            pltpu.VMEM((2, 1, FR), F32),
            pltpu.VMEM((2, 1, FR), F32),
            pltpu.VMEM((2, 1, FR), F32),
            pltpu.VMEM((2, 1, FR), F32),
            dma((7,)),
            dma((len(EARLY),)),
            dma((NZ,)),
            dma((2,)),
            dma,
            dma((NZ,)),
            dma((NZ,)),
            dma((NPIX,)),
            dma((NPIX,)),
            dma,
            dma((2,)),
            dma((4,)),
        ],
        compiler_params=pltpu.CompilerParams(
            collective_id=0, has_side_effects=True, vmem_limit_bytes=48 * 2**20
        ),
    )(library, annulus.reshape(1, ROWS))


def solution(mesh):
    placed = (P("frame", "pix"), P("pix"))
    return jax.shard_map(
        local, mesh=mesh, in_specs=placed, out_specs=P("frame", "pix"), check_vma=False
    )
```

```python
import jax
import jax.numpy as jnp
from jax import lax
from jax.experimental import pallas as pl
from jax.experimental.pallas import tpu as pltpu
from jax.sharding import PartitionSpec as P

PIX = 1536
NZ = 8
NPIX = 8
SL = 24
ROWS = NZ * SL
FR = 384
EARLY = ((0, 8), (8, 16))
NA = (4, 3)
EPS = 1e-06
MESH = pl.DeviceIdType.MESH
F32 = jnp.float32
BF16 = jnp.bfloat16


def device(x, y, z, c):
    return (z * 4 + (y // 2) * 2 + c, x * 2 + y % 2)


def split(v):
    hi = v.astype(BF16)
    return hi, (v - hi.astype(F32)).astype(BF16)


def dot(a, b):
    return lax.dot_general(a, b, (((1,), (0,)), ((), ())), preferred_element_type=F32)


def kernel(
    lib_ref, ann_ref, out_ref,
    piece, rows, cols, acc, left, mu, s1, s2, rmean, rscale,
    snd, move, ag0, swap, ag1, bex, rowsem, rowlow, sibrow, outsem, outsnd,
):
    f = lax.axis_index("frame")
    p = lax.axis_index("pix")
    z, yh, c = f // 4, (f // 2) % 2, f % 2
    x, yl = p // 2, p % 2
    y = 2 * yh + yl

    def at(dx=0, dy=0, dz=0, dc=0):
        return device((x + dx) % 4, (y + dy) % 4, (z + dz) % NZ, (c + dc) % 2)

    sibling = at(dc=1)
    partner = at(dy=2)
    flip = device(x, 2 * yh + 1 - yl, z, c)
    pf = 2 * x + 1 - yl

    barrier = pltpu.get_barrier_semaphore()
    def greet(to):
        pl.semaphore_signal(barrier, inc=1, device_id=to, device_id_type=MESH)

    def target(w):
        return device(z // 2, z % 2 + 2 * yh, w, c)

    for k in range(NPIX):
        @pl.when((k != p) | (z != p))
        def _():
            greet(device(k // 2, 2 * yh + k % 2, p, c))
    for to in (at(dz=1), at(dz=7), at(dx=1), at(dx=3), flip, partner, sibling):
        greet(to)

    band = lax.broadcasted_iota(jnp.int32, (FR, ROWS), 0)
    onehot = jnp.where(band == ann_ref[...], 1.0, 0.0).astype(F32).T.astype(BF16)
    lib = lib_ref[...]
    hi = lib.astype(BF16)
    rest = lib - hi.astype(F32)
    mid = rest.astype(BF16)
    low = (rest - mid.astype(F32)).astype(BF16)
    nt = (((1,), (1,)), ((), ()))
    picked = lax.dot_general(onehot, hi, nt, preferred_element_type=F32)
    picked += lax.dot_general(onehot, mid, nt, preferred_element_type=F32)
    picked += lax.dot_general(onehot, low, nt, preferred_element_type=F32)
    picked = picked.reshape(NZ, SL, FR)
    piece[...] = picked
    rows[c, :, p] = picked

    pl.semaphore_wait(barrier, 7 + NZ - jnp.where(z == p, 1, 0))

    def send(src, dst, out, into, to):
        pltpu.make_async_remote_copy(
            src_ref=src, dst_ref=dst, send_sem=out, recv_sem=into, device_id=to, device_id_type=MESH
        ).start()

    def wait(like, sem):
        pltpu.make_async_copy(like, like, sem).wait()

    def scatter(g):
        span = pl.ds(*EARLY[g])
        for d in (4, 3, 5, 2, 6, 1, 7):
            w = (z + d) % NZ
            send(piece.at[w, span], cols.at[w, 0, p, span], snd.at[0], move.at[g], target(w))

        @pl.when(z != p)
        def _():
            send(piece.at[z, span], cols.at[z, 0, p, span], snd.at[0], move.at[g], target(z))

        @pl.when(z == p)
        def _():
            pltpu.make_async_copy(piece.at[z, span], cols.at[z, 0, p, span], move.at[g]).start()

    def cases(act):
        for core in range(2):
            @pl.when(c == core)
            def _():
                act(pl.ds(0, NA[core]), pl.ds(NA[core], NPIX - NA[core]))

    def cross(j, late, span=pl.ds(0, SL)):
        send(cols.at[j, 0, late, span], cols.at[j, 1, late, span], snd.at[6], bex.at[j], partner)

    def begin(soon, late):
        for g in range(len(EARLY)):
            span = pl.ds(*EARLY[g])
            wait(cols.at[z, 0, :, span], move.at[g])
            part = cols.at[z, 0, late, span]
            for d in (1, 7):
                send(part, part, snd.at[4], ag0.at[z], at(dz=d))
            send(cols.at[z, 0, soon, span], cols.at[z, 1, soon, span], snd.at[3], swap.at[g], partner)
            cross(z, late, span)

    def swapped(g):
        def act(soon, late):
            span = pl.ds(*EARLY[g])
            wait(cols.at[z, 1, soon, span], swap.at[g])
            a = cols.at[z, :, soon, span]
            for d in (1, 7):
                send(a, a, snd.at[5], ag1.at[0, z], at(dz=d))
        cases(act)

    def ends(t):
        return ((z + NZ - t) % NZ, 1), ((z + t) % NZ, 7)

    def arrive_b(t):
        def act(soon, late):
            for i, (j, d) in enumerate(ends(t)):
                b = cols.at[j, 0, late]
                wait(b, ag0.at[j])
                if t == 3:
                    n = late.size // 2
                    b = cols.at[j, 0, pl.ds(late.start + i * n, n if i == 0 else late.size - n)]
                send(b, b, snd.at[4], ag0.at[j], at(dz=d))
                cross(j, late)
        cases(act)

    def arrive_a(t):
        def act(soon, late):
            if t == 1:
                for j, d in ends(t):
                    a = cols.at[j, :, soon]
                    wait(a, ag1.at[0, j])
                    send(a, a, snd.at[5], ag1.at[0, j], at(dz=d))
            elif t == 2:
                for i, (j, d) in enumerate(ends(t)):
                    wait(cols.at[j, :, soon], ag1.at[0, j])
                    for h in (i, 1 - i):
                        a = cols.at[j, h, soon]
                        send(a, a, snd.at[5], ag1.at[h, j], at(dz=d))
            else:
                for k in range(2):
                    for i, (j, d) in enumerate(ends(t)):
                        h = i ^ k
                        a = cols.at[j, h, soon]
                        wait(a, ag1.at[h, j])
                        if k == 0:
                            send(a, a, snd.at[5], ag1.at[h, j], at(dz=d))
        cases(act)

    def arrive_far(soon, late):
        wait(cols.at[far, 0, late], ag0.at[far])
        cross(far, late)

    def crossed(j):
        cases(lambda soon, late: wait(cols.at[j, 1, late], bex.at[j]))

    def arrived(h):
        cases(lambda soon, late: wait(cols.at[far, h, soon], ag1.at[h, far]))

    far = (z + 4) % NZ

    def row(k):
        return rows.at[c, :, k]

    def share(k):
        send(row(k), row(k), snd.at[2], sibrow, sibling)

    def both(src, k):
        for d in (1, 3):
            send(src, row(k), snd.at[1], rowsem.at[k], at(dx=d))

    def pass_on(q):
        left, right = 2 * ((x + 3) % 4) + q, 2 * ((x + 1) % 4) + q
        wait(row(left), rowsem.at[left])
        top = rows.at[c, pl.ds(0, 4), left]
        send(top, top, snd.at[1], rowsem.at[left], at(dx=1))
        share(left)
        wait(row(right), rowsem.at[right])
        low = rows.at[c, pl.ds(4, 4), right]
        send(low, low, snd.at[1], rowlow.at[right], at(dx=3))
        share(right)

    def last(q):
        k = 2 * ((x + 2) % 4) + q
        wait(rows.at[c, pl.ds(0, 4), k], rowsem.at[k])
        wait(rows.at[c, pl.ds(4, 4), k], rowlow.at[k])
        share(k)

    def block(ref, *idx):
        return ref[idx].reshape(ROWS, FR)

    def stats():
        last(1 - yl)
        wait(rows.at[0], sibrow)
        for k in range(2):
            def add(j, tot):
                return tot + jnp.sum(block(rows, k, j), axis=0, keepdims=True)

            mean = lax.fori_loop(0, NZ, add, jnp.zeros((1, FR), F32)) / PIX

            def add2(j, tot):
                v = block(rows, k, j) - mean
                return tot + jnp.sum(v * v, axis=0, keepdims=True)

            sq = lax.fori_loop(0, NZ, add2, jnp.zeros((1, FR), F32))
            rmean[k] = mean
            rscale[k] = 1.0 / jnp.sqrt(sq + EPS)

    def shifted(j, h, first):
        v = block(cols, j, h)
        if first:
            mu[h] = jnp.sum(v, axis=0, keepdims=True) / ROWS
        v = v - mu[h]
        one = jnp.sum(v, axis=0, keepdims=True)
        two = jnp.sum(v * v, axis=0, keepdims=True)
        s1[h] = one if first else s1[h] + one
        s2[h] = two if first else s2[h] + two
        return split(v)

    def unit(k, j):
        return [v.T for v in split((block(rows, k, j) - rmean[k]) * rscale[k])]

    def product(j, hs, first=False, final=False):
        if 1 in hs:
            crossed(j)
        pairs = [shifted(j, h, first) for h in hs]
        xhi, xlo = (jnp.concatenate(v, axis=1) for v in zip(*pairs))
        if final:
            (h,) = hs
            m = s1[h] / PIX
            sq = jnp.maximum(s2[h] - PIX * m * m, 0.0)
            scale = 1.0 / jnp.sqrt(sq + EPS)
            col = pl.multiple_of((2 * (yh if h == 0 else 1 - yh) + c) * FR, 128)
            here = out_ref.at[:, pl.ds(col, FR)]
        for k in (1 - c, c) if final else range(2):
            if final:
                uhi, ulo = left[0, k], left[1, k]
            else:
                uhi, ulo = unit(k, j)
            r = dot(uhi, xhi) + dot(uhi, xlo) + dot(ulo, xhi)
            if final:
                acc[h, k] = (acc[h, k] + r) * scale
                if k is c:
                    copy = pltpu.make_async_copy(acc.at[h, k], here, outsnd.at[2 + h])
                else:
                    copy = pltpu.make_async_remote_copy(
                        src_ref=acc.at[h, k], dst_ref=here, send_sem=outsnd.at[h], recv_sem=outsem.at[h],
                        device_id=sibling, device_id_type=MESH,
                    )
                copy.start()
                copies.append(copy)
                continue
            for i, h in enumerate(hs):
                r_h = r[:, i * FR : (i + 1) * FR]
                acc[h, k] = r_h if first else acc[h, k] + r_h

    def pair(t):
        @pl.loop(0, 2)
        def _(i):
            product((z + jnp.where(i == 0, t, NZ - t)) % NZ, (0, 1))

    copies = []
    for g in range(len(EARLY)):
        scatter(g)
    send(piece, row(p), snd.at[1], rowsem.at[p], flip)
    both(piece, p)
    send(piece, row(p), snd.at[2], sibrow, sibling)
    cases(begin)
    wait(row(pf), rowsem.at[pf])
    both(row(pf), pf)
    share(pf)
    pass_on(yl)
    swapped(0)
    arrive_b(1)
    for g in range(1, len(EARLY)):
        swapped(g)
    pass_on(1 - yl)
    arrive_b(2)
    last(yl)
    arrive_a(1)
    stats()
    product(z, (0, 1), True)
    arrive_b(3)
    pair(1)
    arrive_a(2)
    cases(arrive_far)
    pair(2)
    arrive_a(3)
    pair(3)
    for k in range(2):
        left[0, k], left[1, k] = unit(k, far)
    arrived(0)
    product(far, (0,), final=True)
    arrived(1)
    product(far, (1,), final=True)
    for copy in copies:
        copy.wait()

    wait(cols.at[0, 0, pl.ds(0, 7)], snd.at[0])

    @pl.when(z != p)
    def _():
        wait(piece.at[0], snd.at[0])

    wait(cols.at[pl.ds(0, 7), 0], snd.at[1])
    wait(cols.at[:, 0], snd.at[2])

    def sent(soon, late):
        wait(cols.at[0, 0, soon], snd.at[3])
        wait(cols.at[pl.ds(0, 7), 0, late], snd.at[4])
        wait(cols.at[pl.ds(0, 7), :, soon], snd.at[5])
        wait(cols.at[:, 0, late], snd.at[6])

    cases(sent)


def local(library, annulus):
    dma = pltpu.SemaphoreType.DMA
    return pl.pallas_call(
        kernel,
        out_shape=jax.ShapeDtypeStruct((FR, 4 * FR), F32),
        in_specs=[pl.BlockSpec(memory_space=pltpu.VMEM)] * 2,
        out_specs=pl.BlockSpec(memory_space=pl.ANY),
        scratch_shapes=[
            pltpu.VMEM((NZ, SL, FR), F32),
            pltpu.VMEM((2, NZ, NPIX, SL, FR), F32),
            pltpu.VMEM((NZ, 2, NPIX, SL, FR), F32),
            pltpu.VMEM((2, 2, FR, FR), F32),
            pltpu.VMEM((2, 2, FR, ROWS), BF16),
            pltpu.VMEM((2, 1, FR), F32),
            pltpu.VMEM((2, 1, FR), F32),
            pltpu.VMEM((2, 1, FR), F32),
            pltpu.VMEM((2, 1, FR), F32),
            pltpu.VMEM((2, 1, FR), F32),
            dma((7,)),
            dma((len(EARLY),)),
            dma((NZ,)),
            dma((len(EARLY),)),
            dma((2, NZ)),
            dma((NZ,)),
            dma((NPIX,)),
            dma((NPIX,)),
            dma,
            dma((2,)),
            dma((4,)),
        ],
        compiler_params=pltpu.CompilerParams(
            collective_id=0, has_side_effects=True, vmem_limit_bytes=48 * 2**20
        ),
    )(library, annulus.reshape(1, ROWS))


def solution(mesh):
    placed = (P("frame", "pix"), P("pix"))
    return jax.shard_map(
        local, mesh=mesh, in_specs=placed, out_specs=P("frame", "pix"), check_vma=False
    )
```

```python
import jax
import jax.numpy as jnp
from jax import lax
from jax.experimental import pallas as pl
from jax.experimental.pallas import tpu as pltpu
from jax.sharding import PartitionSpec as P

PIX = 1536
NZ = 8
NPIX = 8
SL = 24
ROWS = NZ * SL
FR = 384
EARLY = ((0, 8), (8, 16))
NA = (4, 3)
EPS = 1e-06
MESH = pl.DeviceIdType.MESH
F32 = jnp.float32
BF16 = jnp.bfloat16


def device(x, y, z, c):
    return (z * 4 + (y // 2) * 2 + c, x * 2 + y % 2)


def split(v):
    hi = v.astype(BF16)
    return hi, (v - hi.astype(F32)).astype(BF16)


def dot(a, b):
    return lax.dot_general(a, b, (((1,), (0,)), ((), ())), preferred_element_type=F32)


def kernel(
    lib_ref, ann_ref, out_ref,
    piece, rows, cols, acc, left, mu, s1, s2, rmean, rscale,
    snd, move, ag0, swap, ag1, bex, rowsem, rowlow, sibrow, outsem, outsnd,
):
    f = lax.axis_index("frame")
    p = lax.axis_index("pix")
    z, yh, c = f // 4, (f // 2) % 2, f % 2
    x, yl = p // 2, p % 2
    y = 2 * yh + yl

    def at(dx=0, dy=0, dz=0, dc=0):
        return device((x + dx) % 4, (y + dy) % 4, (z + dz) % NZ, (c + dc) % 2)

    sibling = at(dc=1)
    partner = at(dy=2)
    flip = device(x, 2 * yh + 1 - yl, z, c)
    pf = 2 * x + 1 - yl

    barrier = pltpu.get_barrier_semaphore()
    def greet(to):
        pl.semaphore_signal(barrier, inc=1, device_id=to, device_id_type=MESH)

    def target(w):
        return device(z // 2, z % 2 + 2 * yh, w, c)

    for k in range(NPIX):
        @pl.when((k != p) | (z != p))
        def _():
            greet(device(k // 2, 2 * yh + k % 2, p, c))
    for to in (at(dz=1), at(dz=7), at(dx=1), at(dx=3), flip, partner, sibling):
        greet(to)

    band = lax.broadcasted_iota(jnp.int32, (ROWS, FR), 1)
    want = jnp.broadcast_to(ann_ref[...], (8, ROWS)).T[:, :1]
    onehot = jnp.where(band == want, 1.0, 0.0).astype(BF16)
    lib = lib_ref[...]
    hi = lib.astype(BF16)
    rest = lib - hi.astype(F32)
    mid = rest.astype(BF16)
    low = (rest - mid.astype(F32)).astype(BF16)
    nt = (((1,), (1,)), ((), ()))
    picked = lax.dot_general(onehot, hi, nt, preferred_element_type=F32)
    picked += lax.dot_general(onehot, mid, nt, preferred_element_type=F32)
    picked += lax.dot_general(onehot, low, nt, preferred_element_type=F32)
    picked = picked.reshape(NZ, SL, FR)
    piece[...] = picked
    rows[c, :, p] = picked

    pl.semaphore_wait(barrier, 7 + NZ - jnp.where(z == p, 1, 0))

    def send(src, dst, out, into, to):
        pltpu.make_async_remote_copy(
            src_ref=src, dst_ref=dst, send_sem=out, recv_sem=into, device_id=to, device_id_type=MESH
        ).start()

    def wait(like, sem):
        pltpu.make_async_copy(like, like, sem).wait()

    def scatter(g):
        span = pl.ds(*EARLY[g])
        for d in (4, 3, 5, 2, 6, 1, 7):
            w = (z + d) % NZ
            send(piece.at[w, span], cols.at[w, 0, p, span], snd.at[0], move.at[g], target(w))

        @pl.when(z != p)
        def _():
            send(piece.at[z, span], cols.at[z, 0, p, span], snd.at[0], move.at[g], target(z))

        @pl.when(z == p)
        def _():
            pltpu.make_async_copy(piece.at[z, span], cols.at[z, 0, p, span], move.at[g]).start()

    def cases(act):
        for core in range(2):
            @pl.when(c == core)
            def _():
                act(pl.ds(0, NA[core]), pl.ds(NA[core], NPIX - NA[core]))

    def cross(j, late, span=pl.ds(0, SL)):
        send(cols.at[j, 0, late, span], cols.at[j, 1, late, span], snd.at[6], bex.at[j], partner)

    def begin(soon, late):
        for g in range(len(EARLY)):
            span = pl.ds(*EARLY[g])
            wait(cols.at[z, 0, :, span], move.at[g])
            part = cols.at[z, 0, late, span]
            for d in (1, 7):
                send(part, part, snd.at[4], ag0.at[z], at(dz=d))
            send(cols.at[z, 0, soon, span], cols.at[z, 1, soon, span], snd.at[3], swap, partner)
            cross(z, late, span)
        pass_a(z, 0, soon, (1, 7))

    def pass_a(j, h, soon, ds):
        a = cols.at[j, h, soon]
        for d in ds:
            send(a, a, snd.at[5], ag1.at[h, j], at(dz=d))

    def swapped(soon, late):
        wait(cols.at[z, 1, soon], swap)
        pass_a(z, 1, soon, (1, 7))

    def ends(t):
        return ((z + NZ - t) % NZ, 1), ((z + t) % NZ, 7)

    def arrive_b(t):
        def act(soon, late):
            for i, (j, d) in enumerate(ends(t)):
                b = cols.at[j, 0, late]
                wait(b, ag0.at[j])
                if t == 3:
                    n = late.size // 2
                    b = cols.at[j, 0, pl.ds(late.start + i * n, n if i == 0 else late.size - n)]
                send(b, b, snd.at[4], ag0.at[j], at(dz=d))
                cross(j, late)
        cases(act)

    def arrive_a(t, h):
        def act(soon, late):
            for i, (j, d) in enumerate(ends(t)):
                wait(cols.at[j, h, soon], ag1.at[h, j])
                if t < 3 or i == h:
                    pass_a(j, h, soon, (d,))
        cases(act)

    def arrive_far(soon, late):
        wait(cols.at[far, 0, late], ag0.at[far])
        cross(far, late)

    def crossed(j):
        cases(lambda soon, late: wait(cols.at[j, 1, late], bex.at[j]))

    def arrived(h):
        cases(lambda soon, late: wait(cols.at[far, h, soon], ag1.at[h, far]))

    far = (z + 4) % NZ

    def row(k):
        return rows.at[c, :, k]

    def share(k):
        send(row(k), row(k), snd.at[2], sibrow, sibling)

    def both(src, k):
        for d in (1, 3):
            send(src, row(k), snd.at[1], rowsem.at[k], at(dx=d))

    def pass_on(q):
        left, right = 2 * ((x + 3) % 4) + q, 2 * ((x + 1) % 4) + q
        wait(row(left), rowsem.at[left])
        top = rows.at[c, pl.ds(0, 4), left]
        send(top, top, snd.at[1], rowsem.at[left], at(dx=1))
        share(left)
        wait(row(right), rowsem.at[right])
        low = rows.at[c, pl.ds(4, 4), right]
        send(low, low, snd.at[1], rowlow.at[right], at(dx=3))
        share(right)

    def last(q):
        k = 2 * ((x + 2) % 4) + q
        wait(rows.at[c, pl.ds(0, 4), k], rowsem.at[k])
        wait(rows.at[c, pl.ds(4, 4), k], rowlow.at[k])
        share(k)

    def block(ref, *idx):
        return ref[idx].reshape(ROWS, FR)

    def stats():
        last(1 - yl)
        wait(rows.at[0], sibrow)
        for k in range(2):
            def add(j, tot):
                return tot + jnp.sum(block(rows, k, j), axis=0, keepdims=True)

            mean = lax.fori_loop(0, NZ, add, jnp.zeros((1, FR), F32)) / PIX

            def add2(j, tot):
                v = block(rows, k, j) - mean
                return tot + jnp.sum(v * v, axis=0, keepdims=True)

            sq = lax.fori_loop(0, NZ, add2, jnp.zeros((1, FR), F32))
            rmean[k] = mean
            rscale[k] = 1.0 / jnp.sqrt(sq + EPS)

    def shifted(j, h, first):
        v = block(cols, j, h)
        if first:
            mu[h] = jnp.sum(v, axis=0, keepdims=True) / ROWS
        v = v - mu[h]
        one = jnp.sum(v, axis=0, keepdims=True)
        two = jnp.sum(v * v, axis=0, keepdims=True)
        s1[h] = one if first else s1[h] + one
        s2[h] = two if first else s2[h] + two
        return split(v)

    def unit(k, j):
        return [v.T for v in split((block(rows, k, j) - rmean[k]) * rscale[k])]

    def product(j, hs, first=False, final=False):
        if 1 in hs:
            crossed(j)
        pairs = [shifted(j, h, first) for h in hs]
        xhi, xlo = (jnp.concatenate(v, axis=1) for v in zip(*pairs))
        if final:
            (h,) = hs
            m = s1[h] / PIX
            sq = jnp.maximum(s2[h] - PIX * m * m, 0.0)
            scale = 1.0 / jnp.sqrt(sq + EPS)
            col = pl.multiple_of((2 * (yh if h == 0 else 1 - yh) + c) * FR, 128)
            here = out_ref.at[:, pl.ds(col, FR)]
        for k in (1 - c, c) if final else range(2):
            if final:
                uhi, ulo = left[0, k], left[1, k]
            else:
                uhi, ulo = unit(k, j)
            r = dot(uhi, xhi) + dot(uhi, xlo) + dot(ulo, xhi)
            if final:
                acc[h, k] = (acc[h, k] + r) * scale
                if k is c:
                    copy = pltpu.make_async_copy(acc.at[h, k], here, outsnd.at[2 + h])
                else:
                    copy = pltpu.make_async_remote_copy(
                        src_ref=acc.at[h, k], dst_ref=here, send_sem=outsnd.at[h], recv_sem=outsem.at[h],
                        device_id=sibling, device_id_type=MESH,
                    )
                copy.start()
                copies.append(copy)
                continue
            for i, h in enumerate(hs):
                r_h = r[:, i * FR : (i + 1) * FR]
                acc[h, k] = r_h if first else acc[h, k] + r_h

    def pair(t):
        @pl.loop(0, 2)
        def _(i):
            product((z + jnp.where(i == 0, t, NZ - t)) % NZ, (0, 1))

    copies = []
    for g in range(len(EARLY)):
        scatter(g)
    send(piece, row(p), snd.at[1], rowsem.at[p], flip)
    both(piece, p)
    send(piece, row(p), snd.at[2], sibrow, sibling)
    cases(begin)
    wait(row(pf), rowsem.at[pf])
    both(row(pf), pf)
    share(pf)
    pass_on(yl)
    arrive_b(1)
    cases(swapped)
    pass_on(1 - yl)
    arrive_b(2)
    last(yl)
    arrive_a(1, 0)
    arrive_a(1, 1)
    stats()
    product(z, (0, 1), True)
    arrive_b(3)
    pair(1)
    arrive_a(2, 0)
    arrive_a(2, 1)
    cases(arrive_far)
    pair(2)
    arrive_a(3, 0)
    arrive_a(3, 1)
    for k in range(2):
        left[0, k], left[1, k] = unit(k, far)
    pair(3)
    arrived(0)
    product(far, (0,), final=True)
    arrived(1)
    product(far, (1,), final=True)
    for copy in copies:
        copy.wait()

    wait(cols.at[0, 0, pl.ds(0, 7)], snd.at[0])

    @pl.when(z != p)
    def _():
        wait(piece.at[0], snd.at[0])

    wait(cols.at[pl.ds(0, 7), 0], snd.at[1])
    wait(cols.at[:, 0], snd.at[2])

    def sent(soon, late):
        wait(cols.at[0, 0, soon], snd.at[3])
        wait(cols.at[pl.ds(0, 7), 0, late], snd.at[4])
        wait(cols.at[pl.ds(0, 7), :, soon], snd.at[5])
        wait(cols.at[:, 0, late], snd.at[6])

    cases(sent)


def local(library, annulus):
    dma = pltpu.SemaphoreType.DMA
    return pl.pallas_call(
        kernel,
        out_shape=jax.ShapeDtypeStruct((FR, 4 * FR), F32),
        in_specs=[pl.BlockSpec(memory_space=pltpu.VMEM)] * 2,
        out_specs=pl.BlockSpec(memory_space=pl.ANY),
        scratch_shapes=[
            pltpu.VMEM((NZ, SL, FR), F32),
            pltpu.VMEM((2, NZ, NPIX, SL, FR), F32),
            pltpu.VMEM((NZ, 2, NPIX, SL, FR), F32),
            pltpu.VMEM((2, 2, FR, FR), F32),
            pltpu.VMEM((2, 2, FR, ROWS), BF16),
            pltpu.VMEM((2, 1, FR), F32),
            pltpu.VMEM((2, 1, FR), F32),
            pltpu.VMEM((2, 1, FR), F32),
            pltpu.VMEM((2, 1, FR), F32),
            pltpu.VMEM((2, 1, FR), F32),
            dma((7,)),
            dma((len(EARLY),)),
            dma((NZ,)),
            dma,
            dma((2, NZ)),
            dma((NZ,)),
            dma((NPIX,)),
            dma((NPIX,)),
            dma,
            dma((2,)),
            dma((4,)),
        ],
        compiler_params=pltpu.CompilerParams(
            collective_id=0, has_side_effects=True, vmem_limit_bytes=48 * 2**20
        ),
    )(library, annulus.reshape(1, ROWS))


def solution(mesh):
    placed = (P("frame", "pix"), P("pix"))
    return jax.shard_map(
        local, mesh=mesh, in_specs=placed, out_specs=P("frame", "pix"), check_vma=False
    )
```

```python
import jax
import jax.numpy as jnp
from jax import lax
from jax.experimental import pallas as pl
from jax.experimental.pallas import tpu as pltpu
from jax.sharding import PartitionSpec as P

PIX = 1536
NZ = 8
NPIX = 8
SL = 24
ROWS = NZ * SL
FR = 384
EARLY = ((0, 8), (8, 16))
NA = (4, 3)
EPS = 1e-06
MESH = pl.DeviceIdType.MESH
F32 = jnp.float32
BF16 = jnp.bfloat16


def device(x, y, z, c):
    return (z * 4 + (y // 2) * 2 + c, x * 2 + y % 2)


def split(v):
    hi = v.astype(BF16)
    return hi, (v - hi.astype(F32)).astype(BF16)


def dot(a, b):
    return lax.dot_general(a, b, (((1,), (0,)), ((), ())), preferred_element_type=F32)


def kernel(
    lib_ref, ann_ref, out_ref,
    piece, rows, cols, acc, left, mu, s1, s2, rmean, rscale,
    snd, move, ag0, swap, ag1, bex, rowsem, rowlow, sibrow, outsem, outsnd,
):
    f = lax.axis_index("frame")
    p = lax.axis_index("pix")
    z, yh, c = f // 4, (f // 2) % 2, f % 2
    x, yl = p // 2, p % 2
    y = 2 * yh + yl

    def at(dx=0, dy=0, dz=0, dc=0):
        return device((x + dx) % 4, (y + dy) % 4, (z + dz) % NZ, (c + dc) % 2)

    sibling = at(dc=1)
    partner = at(dy=2)
    flip = device(x, 2 * yh + 1 - yl, z, c)
    pf = 2 * x + 1 - yl

    barrier = pltpu.get_barrier_semaphore()
    def greet(to):
        pl.semaphore_signal(barrier, inc=1, device_id=to, device_id_type=MESH)

    def target(w):
        return device(z // 2, z % 2 + 2 * yh, w, c)

    for k in range(NPIX):
        @pl.when((k != p) | (z != p))
        def _():
            greet(device(k // 2, 2 * yh + k % 2, p, c))
    for to in (at(dz=1), at(dz=7), at(dx=1), at(dx=3), flip, partner, sibling):
        greet(to)

    band = lax.broadcasted_iota(jnp.int32, (ROWS, FR), 1)
    want = jnp.broadcast_to(ann_ref[...], (8, ROWS)).T[:, :1]
    onehot = jnp.where(band == want, 1.0, 0.0).astype(BF16)
    lib = lib_ref[...]
    hi = lib.astype(BF16)
    rest = lib - hi.astype(F32)
    mid = rest.astype(BF16)
    low = (rest - mid.astype(F32)).astype(BF16)
    nt = (((1,), (1,)), ((), ()))
    picked = lax.dot_general(onehot, hi, nt, preferred_element_type=F32)
    picked += lax.dot_general(onehot, mid, nt, preferred_element_type=F32)
    picked += lax.dot_general(onehot, low, nt, preferred_element_type=F32)
    picked = picked.reshape(NZ, SL, FR)
    piece[...] = picked
    rows[c, :, p] = picked

    pl.semaphore_wait(barrier, 7 + NZ - jnp.where(z == p, 1, 0))

    def send(src, dst, out, into, to):
        pltpu.make_async_remote_copy(
            src_ref=src, dst_ref=dst, send_sem=out, recv_sem=into, device_id=to, device_id_type=MESH
        ).start()

    def wait(like, sem):
        pltpu.make_async_copy(like, like, sem).wait()

    def scatter(g):
        span = pl.ds(*EARLY[g])
        for d in (4, 3, 5, 2, 6, 1, 7):
            w = (z + d) % NZ
            send(piece.at[w, span], cols.at[w, 0, p, span], snd.at[0], move.at[g], target(w))

        @pl.when(z != p)
        def _():
            send(piece.at[z, span], cols.at[z, 0, p, span], snd.at[0], move.at[g], target(z))

        @pl.when(z == p)
        def _():
            pltpu.make_async_copy(piece.at[z, span], cols.at[z, 0, p, span], move.at[g]).start()

    def cases(act):
        for core in range(2):
            @pl.when(c == core)
            def _():
                act(pl.ds(0, NA[core]), pl.ds(NA[core], NPIX - NA[core]))

    def cross(j, late, span=pl.ds(0, SL)):
        send(cols.at[j, 0, late, span], cols.at[j, 1, late, span], snd.at[6], bex.at[j], partner)

    def begin(soon, late):
        for g in range(len(EARLY)):
            span = pl.ds(*EARLY[g])
            wait(cols.at[z, 0, :, span], move.at[g])
            part = cols.at[z, 0, late, span]
            for d in (1, 7):
                send(part, part, snd.at[4], ag0.at[z], at(dz=d))
            send(cols.at[z, 0, soon, span], cols.at[z, 1, soon, span], snd.at[3], swap, partner)
            cross(z, late, span)
            if g == 0:
                part = cols.at[z, 0, soon, span]
                for d in (1, 7):
                    send(part, part, snd.at[5], ag1.at[0, z], at(dz=d))

        span = pl.ds(*EARLY[1])
        part = cols.at[z, 0, soon, span]
        for d in (1, 7):
            send(part, part, snd.at[5], ag1.at[0, z], at(dz=d))

    def pass_a(j, h, soon, ds):
        a = cols.at[j, h, soon]
        for d in ds:
            send(a, a, snd.at[5], ag1.at[h, j], at(dz=d))

    def swapped(soon, late):
        wait(cols.at[z, 1, soon], swap)
        pass_a(z, 1, soon, (1, 7))

    def ends(t):
        return ((z + NZ - t) % NZ, 1), ((z + t) % NZ, 7)

    def arrive_b(t):
        def act(soon, late):
            for i, (j, d) in enumerate(ends(t)):
                b = cols.at[j, 0, late]
                wait(b, ag0.at[j])
                if t == 3:
                    n = late.size // 2
                    b = cols.at[j, 0, pl.ds(late.start + i * n, n if i == 0 else late.size - n)]
                send(b, b, snd.at[4], ag0.at[j], at(dz=d))
                cross(j, late)
        cases(act)

    def arrive_a(t, h):
        def act(soon, late):
            for i, (j, d) in enumerate(ends(t)):
                wait(cols.at[j, h, soon], ag1.at[h, j])
                if t < 3 or i == h:
                    pass_a(j, h, soon, (d,))
        cases(act)

    def arrive_far(soon, late):
        wait(cols.at[far, 0, late], ag0.at[far])
        cross(far, late)

    def crossed(j):
        cases(lambda soon, late: wait(cols.at[j, 1, late], bex.at[j]))

    def arrived(h):
        cases(lambda soon, late: wait(cols.at[far, h, soon], ag1.at[h, far]))

    far = (z + 4) % NZ

    def row(k):
        return rows.at[c, :, k]

    def share(k):
        send(row(k), row(k), snd.at[2], sibrow, sibling)

    def both(src, k):
        for d in (1, 3):
            send(src, row(k), snd.at[1], rowsem.at[k], at(dx=d))

    def pass_on(q):
        left, right = 2 * ((x + 3) % 4) + q, 2 * ((x + 1) % 4) + q
        wait(row(left), rowsem.at[left])
        top = rows.at[c, pl.ds(0, 4), left]
        send(top, top, snd.at[1], rowsem.at[left], at(dx=1))
        share(left)
        wait(row(right), rowsem.at[right])
        low = rows.at[c, pl.ds(4, 4), right]
        send(low, low, snd.at[1], rowlow.at[right], at(dx=3))
        share(right)

    def last(q):
        k = 2 * ((x + 2) % 4) + q
        wait(rows.at[c, pl.ds(0, 4), k], rowsem.at[k])
        wait(rows.at[c, pl.ds(4, 4), k], rowlow.at[k])
        share(k)

    def block(ref, *idx):
        return ref[idx].reshape(ROWS, FR)

    def stats():
        last(1 - yl)
        wait(rows.at[0], sibrow)
        for k in range(2):
            def add(j, tot):
                return tot + jnp.sum(block(rows, k, j), axis=0, keepdims=True)

            mean = lax.fori_loop(0, NZ, add, jnp.zeros((1, FR), F32)) / PIX

            def add2(j, tot):
                v = block(rows, k, j) - mean
                return tot + jnp.sum(v * v, axis=0, keepdims=True)

            sq = lax.fori_loop(0, NZ, add2, jnp.zeros((1, FR), F32))
            rmean[k] = mean
            rscale[k] = 1.0 / jnp.sqrt(sq + EPS)

    def shifted(j, h, first):
        v = block(cols, j, h)
        if first:
            mu[h] = jnp.sum(v, axis=0, keepdims=True) / ROWS
        v = v - mu[h]
        one = jnp.sum(v, axis=0, keepdims=True)
        two = jnp.sum(v * v, axis=0, keepdims=True)
        s1[h] = one if first else s1[h] + one
        s2[h] = two if first else s2[h] + two
        return split(v)

    def unit(k, j):
        return [v.T for v in split((block(rows, k, j) - rmean[k]) * rscale[k])]

    def product(j, hs, first=False, final=False):
        if 1 in hs:
            crossed(j)
        pairs = [shifted(j, h, first) for h in hs]
        xhi, xlo = (jnp.concatenate(v, axis=1) for v in zip(*pairs))
        if final:
            (h,) = hs
            m = s1[h] / PIX
            sq = jnp.maximum(s2[h] - PIX * m * m, 0.0)
            scale = 1.0 / jnp.sqrt(sq + EPS)
            col = pl.multiple_of((2 * (yh if h == 0 else 1 - yh) + c) * FR, 128)
            here = out_ref.at[:, pl.ds(col, FR)]
        for k in (1 - c, c) if final else range(2):
            if final:
                uhi, ulo = left[0, k], left[1, k]
            else:
                uhi, ulo = unit(k, j)
            r = dot(uhi, xhi) + dot(uhi, xlo) + dot(ulo, xhi)
            if final:
                acc[h, k] = (acc[h, k] + r) * scale
                if k is c:
                    copy = pltpu.make_async_copy(acc.at[h, k], here, outsnd.at[2 + h])
                else:
                    copy = pltpu.make_async_remote_copy(
                        src_ref=acc.at[h, k], dst_ref=here, send_sem=outsnd.at[h], recv_sem=outsem.at[h],
                        device_id=sibling, device_id_type=MESH,
                    )
                copy.start()
                copies.append(copy)
                continue
            for i, h in enumerate(hs):
                r_h = r[:, i * FR : (i + 1) * FR]
                acc[h, k] = r_h if first else acc[h, k] + r_h

    def pair(t):
        @pl.loop(0, 2)
        def _(i):
            product((z + jnp.where(i == 0, t, NZ - t)) % NZ, (0, 1))

    copies = []
    for g in range(len(EARLY)):
        scatter(g)
    send(piece, row(p), snd.at[1], rowsem.at[p], flip)
    both(piece, p)
    send(piece, row(p), snd.at[2], sibrow, sibling)
    cases(begin)
    wait(row(pf), rowsem.at[pf])
    both(row(pf), pf)
    share(pf)
    pass_on(yl)
    arrive_b(1)
    cases(swapped)
    pass_on(1 - yl)
    arrive_b(2)
    last(yl)
    arrive_a(1, 0)
    arrive_a(1, 1)
    stats()
    product(z, (0, 1), True)
    arrive_b(3)
    pair(1)
    arrive_a(2, 0)
    arrive_a(2, 1)
    cases(arrive_far)
    pair(2)
    arrive_a(3, 0)
    arrive_a(3, 1)
    for k in range(2):
        left[0, k], left[1, k] = unit(k, far)
    pair(3)
    arrived(0)
    product(far, (0,), final=True)
    arrived(1)
    product(far, (1,), final=True)
    for copy in copies:
        copy.wait()

    wait(cols.at[0, 0, pl.ds(0, 7)], snd.at[0])

    @pl.when(z != p)
    def _():
        wait(piece.at[0], snd.at[0])

    wait(cols.at[pl.ds(0, 7), 0], snd.at[1])
    wait(cols.at[:, 0], snd.at[2])

    def sent(soon, late):
        wait(cols.at[0, 0, soon], snd.at[3])
        wait(cols.at[pl.ds(0, 7), 0, late], snd.at[4])
        wait(cols.at[pl.ds(0, 7), :, soon], snd.at[5])
        wait(cols.at[:, 0, late], snd.at[6])

    cases(sent)


def local(library, annulus):
    dma = pltpu.SemaphoreType.DMA
    return pl.pallas_call(
        kernel,
        out_shape=jax.ShapeDtypeStruct((FR, 4 * FR), F32),
        in_specs=[pl.BlockSpec(memory_space=pltpu.VMEM)] * 2,
        out_specs=pl.BlockSpec(memory_space=pl.ANY),
        scratch_shapes=[
            pltpu.VMEM((NZ, SL, FR), F32),
            pltpu.VMEM((2, NZ, NPIX, SL, FR), F32),
            pltpu.VMEM((NZ, 2, NPIX, SL, FR), F32),
            pltpu.VMEM((2, 2, FR, FR), F32),
            pltpu.VMEM((2, 2, FR, ROWS), BF16),
            pltpu.VMEM((2, 1, FR), F32),
            pltpu.VMEM((2, 1, FR), F32),
            pltpu.VMEM((2, 1, FR), F32),
            pltpu.VMEM((2, 1, FR), F32),
            pltpu.VMEM((2, 1, FR), F32),
            dma((7,)),
            dma((len(EARLY),)),
            dma((NZ,)),
            dma,
            dma((2, NZ)),
            dma((NZ,)),
            dma((NPIX,)),
            dma((NPIX,)),
            dma,
            dma((2,)),
            dma((4,)),
        ],
        compiler_params=pltpu.CompilerParams(
            collective_id=0, has_side_effects=True, vmem_limit_bytes=48 * 2**20
        ),
    )(library, annulus.reshape(1, ROWS))


def solution(mesh):
    placed = (P("frame", "pix"), P("pix"))
    return jax.shard_map(
        local, mesh=mesh, in_specs=placed, out_specs=P("frame", "pix"), check_vma=False
    )
```

```python
import jax
import jax.numpy as jnp
from jax import lax
from jax.experimental import pallas as pl
from jax.experimental.pallas import tpu as pltpu
from jax.sharding import PartitionSpec as P

PIX = 1536
NZ = 8
NPIX = 8
SL = 24
ROWS = NZ * SL
FR = 384
EARLY = ((0, 8), (8, 16))
NA = (4, 3)
EPS = 1e-06
MESH = pl.DeviceIdType.MESH
F32 = jnp.float32
BF16 = jnp.bfloat16


def device(x, y, z, c):
    return (z * 4 + (y // 2) * 2 + c, x * 2 + y % 2)


def split(v):
    hi = v.astype(BF16)
    return hi, (v - hi.astype(F32)).astype(BF16)


def dot(a, b):
    return lax.dot_general(a, b, (((1,), (0,)), ((), ())), preferred_element_type=F32)


def kernel(
    lib_ref, ann_ref, out_ref,
    piece, rows, cols, acc, left, mu, s1, s2, rmean, rscale,
    snd, move, ag0, swap, ag1, bex, rowsem, rowlow, sibrow, outsem, outsnd,
):
    f = lax.axis_index("frame")
    p = lax.axis_index("pix")
    z, yh, c = f // 4, (f // 2) % 2, f % 2
    x, yl = p // 2, p % 2
    y = 2 * yh + yl

    def at(dx=0, dy=0, dz=0, dc=0):
        return device((x + dx) % 4, (y + dy) % 4, (z + dz) % NZ, (c + dc) % 2)

    sibling = at(dc=1)
    partner = at(dy=2)
    flip = device(x, 2 * yh + 1 - yl, z, c)
    pf = 2 * x + 1 - yl

    barrier = pltpu.get_barrier_semaphore()
    def greet(to):
        pl.semaphore_signal(barrier, inc=1, device_id=to, device_id_type=MESH)

    def target(w):
        return device(z // 2, z % 2 + 2 * yh, w, c)

    for k in range(NPIX):
        @pl.when((k != p) | (z != p))
        def _():
            greet(device(k // 2, 2 * yh + k % 2, p, c))
    for to in (at(dz=1), at(dz=7), at(dx=1), at(dx=3), flip, partner, sibling):
        greet(to)

    band = lax.broadcasted_iota(jnp.int32, (ROWS, FR), 1)
    want = jnp.broadcast_to(ann_ref[...], (8, ROWS)).T[:, :1]
    onehot = jnp.where(band == want, 1.0, 0.0).astype(BF16)
    lib = lib_ref[...]
    hi = lib.astype(BF16)
    rest = lib - hi.astype(F32)
    mid = rest.astype(BF16)
    low = (rest - mid.astype(F32)).astype(BF16)
    nt = (((1,), (1,)), ((), ()))
    picked = lax.dot_general(onehot, hi, nt, preferred_element_type=F32)
    picked += lax.dot_general(onehot, mid, nt, preferred_element_type=F32)
    picked += lax.dot_general(onehot, low, nt, preferred_element_type=F32)
    picked = picked.reshape(NZ, SL, FR)
    piece[...] = picked
    rows[c, :, p] = picked

    pl.semaphore_wait(barrier, 7 + NZ - jnp.where(z == p, 1, 0))

    def send(src, dst, out, into, to):
        pltpu.make_async_remote_copy(
            src_ref=src, dst_ref=dst, send_sem=out, recv_sem=into, device_id=to, device_id_type=MESH
        ).start()

    def wait(like, sem):
        pltpu.make_async_copy(like, like, sem).wait()

    def scatter(g):
        span = pl.ds(*EARLY[g])
        for d in (4, 3, 5, 2, 6, 1, 7):
            w = (z + d) % NZ
            send(piece.at[w, span], cols.at[w, 0, p, span], snd.at[0], move.at[g], target(w))

        @pl.when(z != p)
        def _():
            send(piece.at[z, span], cols.at[z, 0, p, span], snd.at[0], move.at[g], target(z))

        @pl.when(z == p)
        def _():
            pltpu.make_async_copy(piece.at[z, span], cols.at[z, 0, p, span], move.at[g]).start()

    def cases(act):
        for core in range(2):
            @pl.when(c == core)
            def _():
                act(pl.ds(0, NA[core]), pl.ds(NA[core], NPIX - NA[core]))

    def cross(j, late, span=pl.ds(0, SL)):
        send(cols.at[j, 0, late, span], cols.at[j, 1, late, span], snd.at[6], bex.at[j], partner)

    def begin(soon, late):
        for g in range(len(EARLY)):
            span = pl.ds(*EARLY[g])
            wait(cols.at[z, 0, :, span], move.at[g])
            part = cols.at[z, 0, late, span]
            for d in (1, 7):
                send(part, part, snd.at[4], ag0.at[z], at(dz=d))
            send(cols.at[z, 0, soon, span], cols.at[z, 1, soon, span], snd.at[3], swap, partner)
            cross(z, late, span)
            if g == 0:
                part = cols.at[z, 0, soon, span]
                for d in (1, 7):
                    send(part, part, snd.at[5], ag1.at[0, z], at(dz=d))

        span = pl.ds(*EARLY[1])
        part = cols.at[z, 0, soon, span]
        for d in (1, 7):
            send(part, part, snd.at[5], ag1.at[0, z], at(dz=d))

    def pass_a(j, h, soon, ds):
        a = cols.at[j, h, soon]
        for d in ds:
            send(a, a, snd.at[5], ag1.at[h, j], at(dz=d))

    def swapped(soon, late):
        wait(cols.at[z, 1, soon], swap)
        pass_a(z, 1, soon, (1, 7))

    def ends(t):
        return ((z + NZ - t) % NZ, 1), ((z + t) % NZ, 7)

    def arrive_b(t):
        def act(soon, late):
            for i, (j, d) in enumerate(ends(t)):
                b = cols.at[j, 0, late]
                wait(b, ag0.at[j])
                if t == 3:
                    n = late.size // 2
                    b = cols.at[j, 0, pl.ds(late.start + i * n, n if i == 0 else late.size - n)]
                send(b, b, snd.at[4], ag0.at[j], at(dz=d))
                cross(j, late)
        cases(act)

    def arrive_a(t, h):
        def act(soon, late):
            for i, (j, d) in enumerate(ends(t)):
                wait(cols.at[j, h, soon], ag1.at[h, j])
                if t < 3 or i == h:
                    pass_a(j, h, soon, (d,))
        cases(act)

    def arrive_far(soon, late):
        wait(cols.at[far, 0, late], ag0.at[far])
        cross(far, late)

    def crossed(j):
        cases(lambda soon, late: wait(cols.at[j, 1, late], bex.at[j]))

    def arrived(h):
        cases(lambda soon, late: wait(cols.at[far, h, soon], ag1.at[h, far]))

    far = (z + 4) % NZ

    def row(k):
        return rows.at[c, :, k]

    def share(k):
        send(row(k), row(k), snd.at[2], sibrow, sibling)

    def both(src, k):
        for d in (1, 3):
            send(src, row(k), snd.at[1], rowsem.at[k], at(dx=d))

    def pass_on(q):
        left, right = 2 * ((x + 3) % 4) + q, 2 * ((x + 1) % 4) + q
        wait(row(left), rowsem.at[left])
        top = rows.at[c, pl.ds(0, 4), left]
        send(top, top, snd.at[1], rowsem.at[left], at(dx=1))
        share(left)
        wait(row(right), rowsem.at[right])
        low = rows.at[c, pl.ds(4, 4), right]
        send(low, low, snd.at[1], rowlow.at[right], at(dx=3))
        share(right)

    def last(q):
        k = 2 * ((x + 2) % 4) + q
        wait(rows.at[c, pl.ds(0, 4), k], rowsem.at[k])
        wait(rows.at[c, pl.ds(4, 4), k], rowlow.at[k])
        share(k)

    def block(ref, *idx):
        return ref[idx].reshape(ROWS, FR)

    def stats():
        last(1 - yl)
        wait(rows.at[0], sibrow)
        for k in range(2):
            def add(j, tot):
                return tot + jnp.sum(block(rows, k, j), axis=0, keepdims=True)

            mean = lax.fori_loop(0, NZ, add, jnp.zeros((1, FR), F32)) / PIX

            def add2(j, tot):
                v = block(rows, k, j) - mean
                return tot + jnp.sum(v * v, axis=0, keepdims=True)

            sq = lax.fori_loop(0, NZ, add2, jnp.zeros((1, FR), F32))
            rmean[k] = mean
            rscale[k] = 1.0 / jnp.sqrt(sq + EPS)

    def shifted(j, h, first):
        v = block(cols, j, h)
        if first:
            mu[h] = jnp.sum(v, axis=0, keepdims=True) / ROWS
        v = v - mu[h]
        one = jnp.sum(v, axis=0, keepdims=True)
        two = jnp.sum(v * v, axis=0, keepdims=True)
        s1[h] = one if first else s1[h] + one
        s2[h] = two if first else s2[h] + two
        return split(v)

    def unit(k, j):
        return [v.T for v in split((block(rows, k, j) - rmean[k]) * rscale[k])]

    def product(j, hs, first=False, final=False):
        if 1 in hs:
            crossed(j)
        pairs = [shifted(j, h, first) for h in hs]
        xhi, xlo = (jnp.concatenate(v, axis=1) for v in zip(*pairs))
        if final:
            (h,) = hs
            m = s1[h] / PIX
            sq = jnp.maximum(s2[h] - PIX * m * m, 0.0)
            scale = 1.0 / jnp.sqrt(sq + EPS)
            col = pl.multiple_of((2 * (yh if h == 0 else 1 - yh) + c) * FR, 128)
            here = out_ref.at[:, pl.ds(col, FR)]
        for k in (1 - c, c) if final else range(2):
            if final:
                uhi, ulo = left[0, k], left[1, k]
            else:
                uhi, ulo = unit(k, j)
            r = dot(uhi, xhi) + dot(uhi, xlo) + dot(ulo, xhi)
            if final:
                acc[h, k] = (acc[h, k] + r) * scale
                if k is c:
                    copy = pltpu.make_async_copy(acc.at[h, k], here, outsnd.at[2 + h])
                else:
                    copy = pltpu.make_async_remote_copy(
                        src_ref=acc.at[h, k], dst_ref=here, send_sem=outsnd.at[h], recv_sem=outsem.at[h],
                        device_id=sibling, device_id_type=MESH,
                    )
                copy.start()
                copies.append(copy)
                continue
            for i, h in enumerate(hs):
                r_h = r[:, i * FR : (i + 1) * FR]
                acc[h, k] = r_h if first else acc[h, k] + r_h

    def pair(t):
        @pl.loop(0, 2)
        def _(i):
            product((z + jnp.where(i == 0, t, NZ - t)) % NZ, (0, 1))

    copies = []
    for g in range(len(EARLY)):
        scatter(g)
    send(piece, row(p), snd.at[1], rowsem.at[p], flip)
    both(piece, p)
    send(piece, row(p), snd.at[2], sibrow, sibling)
    cases(begin)
    wait(row(pf), rowsem.at[pf])
    both(row(pf), pf)
    share(pf)
    pass_on(yl)
    arrive_b(1)
    cases(swapped)
    pass_on(1 - yl)
    arrive_b(2)
    last(yl)
    arrive_a(1, 0)
    arrive_a(1, 1)
    stats()
    product(z, (0, 1), True)
    arrive_b(3)
    pair(1)
    arrive_a(2, 0)
    arrive_a(2, 1)
    cases(arrive_far)
    pair(2)
    arrive_a(3, 0)
    arrive_a(3, 1)
    for k in range(2):
        left[0, k], left[1, k] = unit(k, far)
    pair(3)
    wait(cols.at[0, 0, pl.ds(0, 7)], snd.at[0])

    @pl.when(z != p)
    def _():
        wait(piece.at[0], snd.at[0])

    wait(cols.at[pl.ds(0, 7), 0], snd.at[1])
    wait(cols.at[:, 0], snd.at[2])

    def sent(soon, late):
        wait(cols.at[0, 0, soon], snd.at[3])
        wait(cols.at[pl.ds(0, 7), 0, late], snd.at[4])

    cases(sent)
    arrived(0)
    product(far, (0,), final=True)
    arrived(1)
    product(far, (1,), final=True)
    for copy in copies:
        copy.wait()

    def rest(soon, late):
        wait(cols.at[pl.ds(0, 7), :, soon], snd.at[5])
        wait(cols.at[:, 0, late], snd.at[6])

    cases(rest)


def local(library, annulus):
    dma = pltpu.SemaphoreType.DMA
    return pl.pallas_call(
        kernel,
        out_shape=jax.ShapeDtypeStruct((FR, 4 * FR), F32),
        in_specs=[pl.BlockSpec(memory_space=pltpu.VMEM)] * 2,
        out_specs=pl.BlockSpec(memory_space=pl.ANY),
        scratch_shapes=[
            pltpu.VMEM((NZ, SL, FR), F32),
            pltpu.VMEM((2, NZ, NPIX, SL, FR), F32),
            pltpu.VMEM((NZ, 2, NPIX, SL, FR), F32),
            pltpu.VMEM((2, 2, FR, FR), F32),
            pltpu.VMEM((2, 2, FR, ROWS), BF16),
            pltpu.VMEM((2, 1, FR), F32),
            pltpu.VMEM((2, 1, FR), F32),
            pltpu.VMEM((2, 1, FR), F32),
            pltpu.VMEM((2, 1, FR), F32),
            pltpu.VMEM((2, 1, FR), F32),
            dma((7,)),
            dma((len(EARLY),)),
            dma((NZ,)),
            dma,
            dma((2, NZ)),
            dma((NZ,)),
            dma((NPIX,)),
            dma((NPIX,)),
            dma,
            dma((2,)),
            dma((4,)),
        ],
        compiler_params=pltpu.CompilerParams(
            collective_id=0, has_side_effects=True, vmem_limit_bytes=48 * 2**20
        ),
    )(library, annulus.reshape(1, ROWS))


def solution(mesh):
    placed = (P("frame", "pix"), P("pix"))
    return jax.shard_map(
        local, mesh=mesh, in_specs=placed, out_specs=P("frame", "pix"), check_vma=False
    )
```
